256 devices in a mesh: row: 16 (over y, x), col: 16 (over z, core).
Axes of the slice: x: 4, y: 4, z: 8, core: 2. Of those that a mesh axis runs over, the one named last changes fastest.
Arguments:
- block_input: bfloat16 [1024, 6144], P('col', 'row'), may hold values from -6 to 6
- cotangent: bfloat16 [1024, 6144], P('col', 'row'), may hold values from -6 to 6
- weight_in: bfloat16 [6144, 24576], P('row', 'col'), may hold values from -0.078125 to 0.078125
- weight_out: bfloat16 [24576, 6144], P('col', 'row'), may hold values from -0.0390625 to 0.0390625
Outputs:
- grad_x: float32 [1024, 6144], P('col', 'row')
- grad_in: float32 [6144, 24576], P('row', 'col')
- grad_out: float32 [24576, 6144], P('col', 'row')
The draws below stay inside these ranges and needn't reach their ends.
All inputs are finite; a program needn't handle non-finite values.
Results may differ from the reference program's by a relative error of at most 0.0029.
Values may be sent and summed in bfloat16 or wider, within the bound.
No kernel may reach another device: no remote copies, remote signals or barrier semaphores. Data moves between devices by JAX's collectives and lax.ppermute only.
A program may use at most 128 MiB of HBM per device.

```python
import jax
import jax.numpy as jnp

D = 6144
FF = 24576
TOKENS = 1024


def block_scale(rng, dims, shards, low, high):
    factor_of = 1.0
    for dim, shards_of in shards:
        draws = jax.random.uniform(jax.random.fold_in(jax.random.fold_in(rng, 6), dim), (shards_of,), jnp.float32, low / len(shards), high / len(shards))
        factor_of = factor_of * jnp.repeat(jnp.exp(draws), dims[dim] // shards_of).reshape((-1,) + (1,) * (len(dims) - 1 - dim))
    return factor_of


def bell_draw(stream_key, dims, deviation, reach, shards=(), dtype=jnp.bfloat16):
    values = deviation * jax.random.normal(stream_key, dims, jnp.float32)
    if shards:
        values = values * block_scale(stream_key, dims, shards, -0.22, 0.18)
    return jnp.clip(values, -reach, reach).astype(dtype)


def setup_inputs(seed: int = 0) -> dict:
    streams_of = jax.random.split(jax.random.key(seed), 5)
    block_input = bell_draw(streams_of[0], (TOKENS, D), 1.0, 6.0, ((0, 16), (1, 16)))
    cotangent = bell_draw(streams_of[1], (TOKENS, D), 1.0, 6.0, ((0, 16), (1, 16)))
    weight_in = bell_draw(streams_of[2], (D, FF), D ** -0.5, 0.078125, ((0, 16), (1, 16)))
    weight_out = bell_draw(streams_of[3], (FF, D), FF ** -0.5, 0.0390625, ((0, 16), (1, 16)))
    return {"block_input": block_input, "cotangent": cotangent, "weight_in": weight_in, "weight_out": weight_out}


root_coef = 0.7978845608028654
cubic_coef = 0.044715


def gelu_parts(preact):
    inner = root_coef * (preact + cubic_coef * preact * preact * preact)
    tanh_value = jnp.tanh(inner)
    activation = 0.5 * preact * (1.0 + tanh_value)
    slopes = 0.5 * (1.0 + tanh_value) + 0.5 * preact * (1.0 - tanh_value * tanh_value) * root_coef * (1.0 + 3.0 * cubic_coef * preact * preact)
    return activation, slopes


def reference(block_input, cotangent, weight_in, weight_out):
    tokens_all = block_input.shape[0]
    preact = jnp.dot(block_input, weight_in, preferred_element_type=jnp.float32)
    back_grad = jnp.dot(cotangent, weight_out.T, preferred_element_type=jnp.float32)
    activation, slopes = gelu_parts(preact)
    activation = activation.astype(jnp.bfloat16)
    deltas = (back_grad * slopes).astype(jnp.bfloat16)
    factor = float(tokens_all) ** -0.5
    grad_out = jnp.dot(activation.T, cotangent, preferred_element_type=jnp.float32) * factor
    grad_in = jnp.dot(block_input.T, deltas, preferred_element_type=jnp.float32) * factor
    grad_x = jnp.dot(deltas, weight_in.T, preferred_element_type=jnp.float32)
    return grad_x, grad_in, grad_out
```

```python
import jax
import jax.numpy as jnp
from jax import lax
from jax.sharding import PartitionSpec as P

root_coef = 0.7978845608028654
cubic_coef = 0.044715
f32, f16, bf16 = jnp.float32, jnp.float16, jnp.bfloat16
AXES = ("row", "col")
SIDE, DEPTH = 4, 8
FF_SCALE, X_SCALE = 1024.0, 32.0


def gelu_parts(preact):
    inner = root_coef * (preact + cubic_coef * preact * preact * preact)
    tanh_value = jnp.tanh(inner)
    activation = 0.5 * preact * (1.0 + tanh_value)
    slopes = 0.5 * (1.0 + tanh_value) + 0.5 * preact * (
        1.0 - tanh_value * tanh_value
    ) * root_coef * (1.0 + 3.0 * cubic_coef * preact * preact)
    return (activation, slopes)


def trans_dot(left, right):
    return lax.dot_general(
        left, right, (((0,), (0,)), ((), ())), preferred_element_type=f32
    )


def last_dot(left, right):
    return lax.dot_general(
        left, right, (((1,), (1,)), ((), ())), preferred_element_type=f32
    )


def encode(value, scale):
    size = jnp.abs(value)
    return (value * (lax.rsqrt(jnp.maximum(size, 1e-30)) * scale)).astype(f16)


def decode(code, scale):
    code = code.astype(f32)
    return code * jnp.abs(code) * (1.0 / (scale * scale))


def index(y, x, z, core):
    return ((y % SIDE) * SIDE + x % SIDE) * 2 * DEPTH + (z % DEPTH) * 2 + core


def all_chips():
    return [
        (y, x, z, c)
        for y in range(SIDE)
        for x in range(SIDE)
        for z in range(DEPTH)
        for c in range(2)
    ]


def send_plane(value, axis, step):
    perm = []
    for y, x, z, c in all_chips():
        along_y = (axis == 0) == (c == 0)
        to = (y + step, x) if along_y else (y, x + step)
        perm.append((index(y, x, z, c), index(*to, z, c)))
    return lax.ppermute(value, AXES, perm)


def send_z(value, step):
    perm = [
        (index(y, x, z, c), index(y, x, z + (step if c == 0 else -step), c))
        for y, x, z, c in all_chips()
    ]
    return lax.ppermute(value, AXES, perm)


def swap(value):
    perm = [(index(y, x, z, c), index(y, x, z, 1 - c)) for y, x, z, c in all_chips()]
    return lax.ppermute(value, AXES, perm)


def gather_z(own):
    other = swap(own)
    block = jnp.concatenate([own, other], 0)
    got = []
    for _ in range(3):
        block = send_z(block, 1)
        got.append(block)
    got.append(send_z(block[: own.shape[0]], 1))
    mine = jnp.concatenate(got, 0)
    theirs = swap(mine)
    return jnp.concatenate([own, mine, other, theirs], 0)


def scatter_z(total, rows, scale):
    half = total.shape[0] // 2
    theirs = swap(encode(total[half:], scale))
    mine = total[:half] + decode(theirs, scale)
    parts = []
    for k in (4, 3, 2, 1):
        low = rows + (k - 1) * 2 * rows
        high = half if k == 4 else low + 2 * rows
        parts.append(decode(send_z(encode(mine[low:high], scale), -k), scale))
    other = parts[1][rows:] + parts[2][rows:] + parts[3][rows:]
    got = decode(swap(encode(other, scale)), scale)
    return mine[:rows] + parts[0] + parts[1][:rows] + parts[2][:rows] + parts[3][:rows] + got


def scatter_plane(product, rows, scale):
    size = SIDE * rows
    mid = size // 2
    far = product(2)
    via_up = send_plane(encode(far[:mid], scale), 0, 1)
    via_down = send_plane(encode(far[mid:], scale), 0, -1)
    up = product(1)
    up = jnp.concatenate(
        [encode(up[:mid] + decode(via_up, scale), scale), encode(up[mid:], scale)], 0
    )
    from_below = send_plane(up, 0, 1)
    down = product(3)
    down = jnp.concatenate(
        [encode(down[:mid], scale), encode(down[mid:] + decode(via_down, scale), scale)], 0
    )
    from_above = send_plane(down, 0, -1)
    line = product(0) + decode(from_below, scale) + decode(from_above, scale)
    total = line[:rows]
    for d in (2, 1, 3):
        total = total + decode(
            send_plane(encode(line[d * rows : (d + 1) * rows], scale), 1, d), scale
        )
    return total


def gather_plane(own):
    got = {d: send_plane(own, 1, -d) for d in (2, 1, 3)}
    line = jnp.concatenate([own, got[1], got[2], got[3]], 0)
    mid = line.shape[0] // 2
    up = send_plane(line, 0, -1)
    down = send_plane(line, 0, 1)
    far_up = send_plane(up[:mid], 0, -1)
    far_down = send_plane(down[mid:], 0, 1)
    return jnp.concatenate([line, up, far_up, far_down, down], 0)


def roll_blocks(value, first, second, rows):
    n = value.shape[1]
    size = SIDE * rows
    twice = jnp.concatenate([value, value], 0)
    value = lax.dynamic_slice(twice, (first * size, 0), value.shape)
    value = value.reshape(SIDE, size, n)
    twice = jnp.concatenate([value, value], 1)
    value = lax.dynamic_slice(twice, (0, second * rows, 0), value.shape)
    return value.reshape(SIDE * size, n)


def on_device(block_input, cotangent, weight_in, weight_out):
    rows, features = block_input.shape
    place = lax.axis_index("row")
    core = lax.axis_index("col") % 2
    y, x = place // SIDE, place % SIDE
    first, second = jnp.where(core == 0, y, x), jnp.where(core == 0, x, y)

    both = gather_z(jnp.concatenate([block_input, cotangent], 1))
    both = roll_blocks(both, first, second, rows)
    inputs_all, cot_all = both[:, :features], both[:, features:]
    size = SIDE * rows
    factor = float(inputs_all.shape[0]) ** (-0.5)

    preact = scatter_plane(
        lambda d: jnp.dot(inputs_all[d * size : (d + 1) * size], weight_in, preferred_element_type=f32),
        rows,
        FF_SCALE,
    )
    back_grad = scatter_plane(
        lambda d: last_dot(cot_all[d * size : (d + 1) * size], weight_out), rows, FF_SCALE
    )
    activation, slopes = gelu_parts(preact)
    act_all = gather_plane(activation.astype(bf16))
    deltas_all = gather_plane((back_grad * slopes).astype(bf16))
    grad_out = trans_dot(act_all, cot_all) * factor
    grad_in = trans_dot(inputs_all, deltas_all) * factor
    partial = last_dot(deltas_all, weight_in)
    partial = roll_blocks(partial, (SIDE - first) % SIDE, (SIDE - second) % SIDE, rows)
    grad_x = scatter_z(partial, rows, X_SCALE)
    return (grad_x, grad_in, grad_out)


def solution(mesh):
    in_specs = (P("col", "row"), P("col", "row"), P("row", "col"), P("col", "row"))
    out_specs = (P("col", "row"), P("row", "col"), P("col", "row"))
    return jax.shard_map(
        on_device, mesh=mesh, in_specs=in_specs, out_specs=out_specs, check_vma=False
    )
```

```python
import jax
import jax.numpy as jnp
from jax import lax
from jax.experimental import pallas as pl
from jax.experimental.pallas import tpu as pltpu
from jax.sharding import PartitionSpec as P

root_coef = 0.7978845608028654
cubic_coef = 0.044715
f32, f16, bf16 = jnp.float32, jnp.float16, jnp.bfloat16
AXES = ("row", "col")
SIDE, DEPTH = 4, 8
FF_SCALE, X_SCALE = 1024.0, 32.0


def gelu_parts(preact):
    inner = root_coef * (preact + cubic_coef * preact * preact * preact)
    tanh_value = jnp.tanh(inner)
    activation = 0.5 * preact * (1.0 + tanh_value)
    slopes = 0.5 * (1.0 + tanh_value) + 0.5 * preact * (
        1.0 - tanh_value * tanh_value
    ) * root_coef * (1.0 + 3.0 * cubic_coef * preact * preact)
    return (activation, slopes)


def encode(value, scale):
    size = jnp.abs(value)
    return (value * (lax.rsqrt(jnp.maximum(size, 1e-30)) * scale)).astype(f16)


def decode(code, scale):
    code = code.astype(f32)
    return code * jnp.abs(code) * (1.0 / (scale * scale))


def index(y, x, z, core):
    return ((y % SIDE) * SIDE + x % SIDE) * 2 * DEPTH + (z % DEPTH) * 2 + core


def all_chips():
    return [
        (y, x, z, c)
        for y in range(SIDE)
        for x in range(SIDE)
        for z in range(DEPTH)
        for c in range(2)
    ]


def send_plane(value, axis, step):
    perm = []
    for y, x, z, c in all_chips():
        along_y = (axis == 0) == (c == 0)
        to = (y + step, x) if along_y else (y, x + step)
        perm.append((index(y, x, z, c), index(*to, z, c)))
    return lax.ppermute(value, AXES, perm)


def send_z(value, step):
    perm = [
        (index(y, x, z, c), index(y, x, z + (step if c == 0 else -step), c))
        for y, x, z, c in all_chips()
    ]
    return lax.ppermute(value, AXES, perm)


def swap(value):
    perm = [(index(y, x, z, c), index(y, x, z, 1 - c)) for y, x, z, c in all_chips()]
    return lax.ppermute(value, AXES, perm)


def call(kernel, outs, *operands, scalars=(), **rest):
    specs = [pl.BlockSpec(memory_space=pltpu.SMEM)] * len(scalars)
    specs += [pl.BlockSpec(memory_space=pltpu.VMEM)] * len(operands)
    return pl.pallas_call(
        kernel,
        out_shape=outs,
        in_specs=specs,
        out_specs=pl.BlockSpec(memory_space=pltpu.VMEM),
        compiler_params=pltpu.CompilerParams(vmem_limit_bytes=24 << 20),
        **rest,
    )(*scalars, *operands)


def rolled_block(place, block):
    to_first = lax.rem(block // SIDE + SIDE - place[0], SIDE)
    to_second = lax.rem(block % SIDE + SIDE - place[1], SIDE)
    return to_first * SIDE + to_second


def roll_in(place, pieces, keep):
    _, _, n = pieces[0].shape
    total = sum(high - low for low, high in keep)
    size = total // (SIDE * SIDE)

    def kernel(place_ref, *refs):
        out = refs[-1]
        start = 0
        for ref, (low, high) in zip(refs[:-1], keep):
            for row in range(low, high, size):
                block = (start + row - low) // size
                to = pl.multiple_of(rolled_block(place_ref, block) * size, size)
                for which in range(2):
                    out[which, pl.ds(to, size), :] = ref[which, row : row + size, :]
            start += high - low

    out = jax.ShapeDtypeStruct((2, total, n), pieces[0].dtype)
    cost = pl.CostEstimate(flops=0, transcendentals=0, bytes_accessed=8 * total * n)
    return call(kernel, out, *pieces, scalars=(place,), cost_estimate=cost)


def roll_back(place, pieces):
    rows, n = pieces[0].shape
    size = rows // SIDE
    total = SIDE * rows

    def kernel(place_ref, *refs):
        out = refs[-1]
        for d, ref in enumerate(refs[:-1]):
            for e in range(SIDE):
                first = lax.rem(place_ref[0] + d, SIDE)
                second = lax.rem(place_ref[1] + e, SIDE)
                to = pl.multiple_of((first * SIDE + second) * size, size)
                out[pl.ds(to, size), :] = ref[e * size : (e + 1) * size, :]

    out = jax.ShapeDtypeStruct((total, n), pieces[0].dtype)
    cost = pl.CostEstimate(flops=0, transcendentals=0, bytes_accessed=8 * total * n)
    return call(kernel, out, *pieces, scalars=(place,), cost_estimate=cost)


def pair_dot(left, right):
    return lax.dot_general(
        left, right, (((2,), (1,)), ((0,), (0,))), preferred_element_type=f32
    )


def scatter_plane(tokens, weights):
    size = tokens.shape[1] // SIDE
    rows = size // SIDE
    product = lambda d: pair_dot(tokens[:, d * size : (d + 1) * size], weights)
    far = encode(product(2), FF_SCALE)
    via_up = decode(send_plane(far[:1], 0, 1), FF_SCALE)
    via_down = decode(send_plane(far[1:], 0, -1), FF_SCALE)
    none = jnp.zeros_like(via_up)
    up = product(1) + jnp.concatenate([via_up, none], 0)
    down = product(3) + jnp.concatenate([none, via_down], 0)
    from_below = send_plane(encode(up, FF_SCALE), 0, 1)
    from_above = send_plane(encode(down, FF_SCALE), 0, -1)
    line = product(0) + decode(from_below, FF_SCALE) + decode(from_above, FF_SCALE)
    total = line[:, :rows]
    for d in (2, 1, 3):
        part = encode(line[:, d * rows : (d + 1) * rows], FF_SCALE)
        total = total + decode(send_plane(part, 1, d), FF_SCALE)
    return total


def gather_plane(own):
    got = {d: send_plane(own, 1, -d) for d in (2, 1, 3)}
    line = jnp.concatenate([own, got[1], got[2], got[3]], 1)
    up = send_plane(line, 0, -1)
    down = send_plane(line, 0, 1)
    far_up = send_plane(up[0], 0, -1)
    far_down = send_plane(down[1], 0, 1)
    return [line[0], up[0], far_up, down[0]], [line[1], up[1], far_down, down[1]]


def grad_kernel(pieces, tokens, swapped, factor):
    count = len(pieces)
    rows, hidden = pieces[0].shape
    total, features = count * rows, tokens[0].shape[1]
    tile = hidden // 3

    def kernel(*refs):
        out = refs[-1]
        wide = jnp.concatenate([ref[...] for ref in refs[:count]], 0)
        slim = jnp.concatenate([ref[...] for ref in refs[count:-1]], 0)
        left, right = (slim, wide) if swapped else (wide, slim)
        out[...] = (
            lax.dot_general(left, right, (((0,), (0,)), ((), ())), preferred_element_type=f32)
            * factor
        )

    in_specs = [pl.BlockSpec((rows, tile), lambda i: (0, i))] * count
    in_specs += [pl.BlockSpec(t.shape, lambda i: (0, 0)) for t in tokens]
    if swapped:
        out_spec, out = pl.BlockSpec((features, tile), lambda i: (0, i)), (features, hidden)
    else:
        out_spec, out = pl.BlockSpec((tile, features), lambda i: (i, 0)), (hidden, features)
    return pl.pallas_call(
        kernel,
        grid=(3,),
        in_specs=in_specs,
        out_specs=out_spec,
        out_shape=jax.ShapeDtypeStruct(out, f32),
        compiler_params=pltpu.CompilerParams(vmem_limit_bytes=24 << 20),
        cost_estimate=pl.CostEstimate(
            flops=2 * total * features * hidden,
            transcendentals=0,
            bytes_accessed=2 * total * (features + hidden) + 4 * features * hidden,
        ),
    )(*pieces, *tokens)


def on_device(block_input, cotangent, weight_in, weight_out):
    rows, _ = block_input.shape
    row = lax.axis_index("row")
    core = lax.axis_index("col") % 2
    y, x = row // SIDE, row % SIDE
    place = jnp.where(core == 0, jnp.stack([y, x]), jnp.stack([x, y])).astype(jnp.int32)
    weights = jnp.stack([weight_in, weight_out.T])
    factor = float(rows * 2 * DEPTH) ** (-0.5)
    code = lambda value: encode(value, X_SCALE)
    value = lambda code: decode(code, X_SCALE)

    own = jnp.stack([block_input, cotangent])
    other = swap(own)
    chip = jnp.concatenate([own, other], 1)
    one, two = send_z(chip, 1), send_z(chip, 2)
    other_one, other_two = swap(one), swap(two)
    three, four = send_z(two, 1), send_z(two[:, :rows], 2)
    other_three, other_four = swap(three), swap(four)
    r = rows
    streams = [
        roll_in(
            place,
            (own, one, two, other, other_one, other_two),
            ((0, r), (0, 2 * r), (0, r)) * 2,
        ),
        roll_in(
            place,
            (two, three, four, other_two, other_three, other_four),
            ((r, 2 * r), (0, 2 * r), (0, r)) * 2,
        ),
    ]

    acts, deltas, partials = [], [], []
    for tokens in streams:
        preact, back_grad = scatter_plane(tokens, weights)
        activation, slopes = gelu_parts(preact)
        pair = jnp.stack([activation.astype(bf16), (back_grad * slopes).astype(bf16)])
        act_pieces, delta_pieces = gather_plane(pair)
        acts += act_pieces
        deltas += delta_pieces
        products = [
            lax.dot_general(p, weight_in, (((1,), (1,)), ((), ())), preferred_element_type=f32)
            for p in delta_pieces
        ]
        partials.append(roll_back(place, products))

    half = 4 * r
    near = partials[0][:half] + value(swap(code(partials[0][half:])))
    from_one = value(send_z(code(near[r : 3 * r]), -1))
    from_two = value(send_z(code(near[3 * r :]), -2))
    deep = partials[1][:half] + value(swap(code(partials[1][half:])))
    from_four = value(send_z(code(deep[3 * r :]), -4))
    from_three = value(send_z(code(deep[r : 3 * r]), -3))
    others_two = value(send_z(code(deep[:r]), -2))
    others = value(swap(code(from_one[r:] + others_two + from_three[r:])))
    grad_x = near[:r] + from_one[:r] + from_two + from_three[:r] + from_four + others

    inputs, cots = [s[0] for s in streams], [s[1] for s in streams]
    grad_out = grad_kernel(acts, cots, False, factor)
    grad_in = grad_kernel(deltas, inputs, True, factor)
    return (grad_x, grad_in, grad_out)


def solution(mesh):
    in_specs = (P("col", "row"), P("col", "row"), P("row", "col"), P("col", "row"))
    out_specs = (P("col", "row"), P("row", "col"), P("col", "row"))
    return jax.shard_map(
        on_device, mesh=mesh, in_specs=in_specs, out_specs=out_specs, check_vma=False
    )
```

```python
import jax
import jax.numpy as jnp
from jax import lax
from jax.experimental import pallas as pl
from jax.experimental.pallas import tpu as pltpu
from jax.sharding import PartitionSpec as P

root_coef = 0.7978845608028654
cubic_coef = 0.044715
f32, f16, bf16 = jnp.float32, jnp.float16, jnp.bfloat16
AXES = ("row", "col")
SIDE, DEPTH = 4, 8
FF_SCALE, X_SCALE = 1024.0, 32.0
LONG = pl.CostEstimate(flops=20_000_000_000, transcendentals=0, bytes_accessed=0)


def gelu_parts(preact):
    inner = root_coef * (preact + cubic_coef * preact * preact * preact)
    tanh_value = jnp.tanh(inner)
    activation = 0.5 * preact * (1.0 + tanh_value)
    slopes = 0.5 * (1.0 + tanh_value) + 0.5 * preact * (
        1.0 - tanh_value * tanh_value
    ) * root_coef * (1.0 + 3.0 * cubic_coef * preact * preact)
    return (activation, slopes)


def encode(value, scale):
    size = jnp.abs(value)
    return (value * (lax.rsqrt(jnp.maximum(size, 1e-30)) * scale)).astype(f16)


def decode(code, scale):
    code = code.astype(f32)
    return code * jnp.abs(code) * (1.0 / (scale * scale))


def index(y, x, z, core):
    return ((y % SIDE) * SIDE + x % SIDE) * 2 * DEPTH + (z % DEPTH) * 2 + core


def all_chips():
    return [
        (y, x, z, c)
        for y in range(SIDE)
        for x in range(SIDE)
        for z in range(DEPTH)
        for c in range(2)
    ]


def send_plane(value, axis, step):
    perm = []
    for y, x, z, c in all_chips():
        along_y = (axis == 0) == (c == 0)
        to = (y + step, x) if along_y else (y, x + step)
        perm.append((index(y, x, z, c), index(*to, z, c)))
    return lax.ppermute(value, AXES, perm)


def send_z(value, step):
    perm = [
        (index(y, x, z, c), index(y, x, z + (step if c == 0 else -step), c))
        for y, x, z, c in all_chips()
    ]
    return lax.ppermute(value, AXES, perm)


def swap(value):
    perm = [(index(y, x, z, c), index(y, x, z, 1 - c)) for y, x, z, c in all_chips()]
    return lax.ppermute(value, AXES, perm)


def call(kernel, outs, *operands, scalars=(), **rest):
    specs = [pl.BlockSpec(memory_space=pltpu.SMEM)] * len(scalars)
    specs += [pl.BlockSpec(memory_space=pltpu.VMEM)] * len(operands)
    return pl.pallas_call(
        kernel,
        out_shape=outs,
        in_specs=specs,
        out_specs=pl.BlockSpec(memory_space=pltpu.VMEM),
        compiler_params=pltpu.CompilerParams(vmem_limit_bytes=24 << 20),
        **rest,
    )(*scalars, *operands)


def rolled_block(place, block):
    to_first = lax.rem(block // SIDE + SIDE - place[0], SIDE)
    to_second = lax.rem(block % SIDE + SIDE - place[1], SIDE)
    return to_first * SIDE + to_second


def roll_in(place, pieces, keep):
    _, _, n = pieces[0].shape
    total = sum(high - low for low, high in keep)
    size = total // (SIDE * SIDE)

    def kernel(place_ref, *refs):
        out = refs[-1]
        start = 0
        for ref, (low, high) in zip(refs[:-1], keep):
            for row in range(low, high, size):
                block = (start + row - low) // size
                to = pl.multiple_of(rolled_block(place_ref, block) * size, size)
                for which in range(2):
                    out[which, pl.ds(to, size), :] = ref[which, row : row + size, :]
            start += high - low

    out = jax.ShapeDtypeStruct((2, total, n), pieces[0].dtype)
    return call(kernel, out, *pieces, scalars=(place,), cost_estimate=LONG)


def roll_back(place, pieces):
    rows, n = pieces[0].shape
    size = rows // SIDE
    total = SIDE * rows

    def kernel(place_ref, *refs):
        out = refs[-1]
        for d, ref in enumerate(refs[:-1]):
            for e in range(SIDE):
                first = lax.rem(place_ref[0] + d, SIDE)
                second = lax.rem(place_ref[1] + e, SIDE)
                to = pl.multiple_of((first * SIDE + second) * size, size)
                out[pl.ds(to, size), :] = ref[e * size : (e + 1) * size, :]

    out = jax.ShapeDtypeStruct((total, n), pieces[0].dtype)
    return call(kernel, out, *pieces, scalars=(place,), cost_estimate=LONG)


def pair_dot(left, right):
    return lax.dot_general(
        left, right, (((2,), (1,)), ((0,), (0,))), preferred_element_type=f32
    )


def after(values, *others):
    def kernel(*refs):
        del refs

    return pl.pallas_call(
        kernel,
        out_shape=[jax.ShapeDtypeStruct(v.shape, v.dtype) for v in values],
        in_specs=[pl.BlockSpec(memory_space=pl.ANY)] * (len(values) + len(others)),
        out_specs=[pl.BlockSpec(memory_space=pl.ANY)] * len(values),
        input_output_aliases={i: i for i in range(len(values))},
        cost_estimate=LONG,
    )(*values, *others)


def first_products(tokens, weights, size):
    far = encode(pair_dot(tokens[:, 2 * size : 3 * size], weights), FF_SCALE)
    return far, send_plane(far[:1], 0, 1), send_plane(far[1:], 0, -1)


def second_products(tokens, weights, size, via_up, via_down):
    product = lambda d: pair_dot(tokens[:, d * size : (d + 1) * size], weights)
    none = jnp.zeros_like(via_up)
    up = encode(product(1) + jnp.concatenate([via_up, none], 0), FF_SCALE)
    down = encode(product(3) + jnp.concatenate([none, via_down], 0), FF_SCALE)
    return send_plane(up, 0, 1), send_plane(down, 0, -1)


def third_products(tokens, weights, size, from_below, from_above):
    line = pair_dot(tokens[:, :size], weights)
    line = line + decode(from_below, FF_SCALE) + decode(from_above, FF_SCALE)
    rows = size // SIDE
    parts = {d: encode(line[:, d * rows : (d + 1) * rows], FF_SCALE) for d in (2, 1, 3)}
    return line, {d: send_plane(part, 1, d) for d, part in parts.items()}


def hidden_pair(line, parts):
    total = line[:, : line.shape[1] // SIDE]
    for d in (2, 1, 3):
        total = total + decode(parts[d], FF_SCALE)
    activation, slopes = gelu_parts(total[0])
    return jnp.stack([activation.astype(bf16), (total[1] * slopes).astype(bf16)])


def gather_second(own):
    return {d: send_plane(own, 1, -d) for d in (2, 1, 3)}


def gather_first(own, got):
    line = jnp.concatenate([own, got[1], got[2], got[3]], 1)
    return line, send_plane(line, 0, -1), send_plane(line, 0, 1)


def last(left, right):
    return lax.dot_general(left, right, (((1,), (1,)), ((), ())), preferred_element_type=f32)


def grad_kernel(pieces, tokens, swapped, factor):
    count = len(pieces)
    rows, hidden = pieces[0].shape
    total, features = count * rows, tokens[0].shape[1]
    tile = hidden // 3

    def kernel(*refs):
        out = refs[-1]
        wide = jnp.concatenate([ref[...] for ref in refs[:count]], 0)
        slim = jnp.concatenate([ref[...] for ref in refs[count:-1]], 0)
        left, right = (slim, wide) if swapped else (wide, slim)
        out[...] = (
            lax.dot_general(left, right, (((0,), (0,)), ((), ())), preferred_element_type=f32)
            * factor
        )

    in_specs = [pl.BlockSpec((rows, tile), lambda i: (0, i))] * count
    in_specs += [pl.BlockSpec(t.shape, lambda i: (0, 0)) for t in tokens]
    if swapped:
        out_spec, out = pl.BlockSpec((features, tile), lambda i: (0, i)), (features, hidden)
    else:
        out_spec, out = pl.BlockSpec((tile, features), lambda i: (i, 0)), (hidden, features)
    return pl.pallas_call(
        kernel,
        grid=(3,),
        in_specs=in_specs,
        out_specs=out_spec,
        out_shape=jax.ShapeDtypeStruct(out, f32),
        compiler_params=pltpu.CompilerParams(vmem_limit_bytes=24 << 20),
        cost_estimate=pl.CostEstimate(
            flops=2 * total * features * hidden,
            transcendentals=0,
            bytes_accessed=2 * total * (features + hidden) + 4 * features * hidden,
        ),
    )(*pieces, *tokens)


def on_device(block_input, cotangent, weight_in, weight_out):
    rows, _ = block_input.shape
    row = lax.axis_index("row")
    core = lax.axis_index("col") % 2
    y, x = row // SIDE, row % SIDE
    place = jnp.where(core == 0, jnp.stack([y, x]), jnp.stack([x, y])).astype(jnp.int32)
    factor = float(rows * 2 * DEPTH) ** (-0.5)
    code = lambda value: encode(value, X_SCALE)
    value = lambda code: decode(code, X_SCALE)

    own = jnp.stack([block_input, cotangent])
    other = swap(own)
    chip = jnp.concatenate([own, other], 1)
    one = send_z(chip, 1)
    chip, weight_back = lax.optimization_barrier((chip, weight_out.T))
    weights = jnp.stack([weight_in, weight_back])
    two = send_z(chip, 2)
    other_one, other_two = swap(one), swap(two)
    three, four = send_z(two, 1), send_z(two[:, :rows], 2)
    r = rows
    size = 2 * r
    tokens_a = roll_in(
        place,
        (own, one, two, other, other_one, other_two),
        ((0, r), (0, 2 * r), (0, r)) * 2,
    )
    _, via_up_a, via_down_a = first_products(tokens_a, weights, size)
    three, four = after((three, four), tokens_a)
    other_three, other_four = swap(three), swap(four)
    tokens_b = roll_in(
        place,
        (two, three, four, other_two, other_three, other_four),
        ((r, 2 * r), (0, 2 * r), (0, r)) * 2,
    )
    _, via_up_b, via_down_b = first_products(tokens_b, weights, size)
    (tokens_a,) = after((tokens_a,), tokens_b)
    whole = lambda code: decode(code, FF_SCALE)
    below_a, above_a = second_products(tokens_a, weights, size, whole(via_up_a), whole(via_down_a))
    via_up_b, via_down_b = whole(via_up_b), whole(via_down_b)
    below_b, above_b = second_products(tokens_b, weights, size, via_up_b, via_down_b)
    (tokens_a,) = after((tokens_a,), via_up_b, via_down_b)
    place_a, parts_a = third_products(tokens_a, weights, size, below_a, above_a)
    pair_a = hidden_pair(place_a, parts_a)
    got_a = gather_second(pair_a)
    (tokens_b,) = after((tokens_b,), pair_a)
    place_b, parts_b = third_products(tokens_b, weights, size, below_b, above_b)
    (got_a[1],) = after((got_a[1],), place_b)
    line_a, up_a, down_a = gather_first(pair_a, got_a)
    (place_b,) = after((place_b,), line_a)
    pair_b = hidden_pair(place_b, parts_b)
    got_b = gather_second(pair_b)
    far_up_a, far_down_a = send_plane(up_a[0], 0, -1), send_plane(down_a[1], 0, 1)
    (got_b[1],) = after((got_b[1],), up_a, down_a)
    line_b, up_b, down_b = gather_first(pair_b, got_b)
    (far_down_a,) = after((far_down_a,), line_b)
    deltas = [line_a[1], up_a[1], far_down_a, down_a[1]]
    partial = roll_back(place, [last(p, weight_in) for p in deltas])
    half = 4 * r
    near = partial[:half] + value(swap(code(partial[half:])))
    near_one, near_two = code(near[r : 3 * r]), code(near[3 * r :])
    from_one, from_two = send_z(near_one, -1), send_z(near_two, -2)
    (up_b,) = after((up_b,), near)
    far_up_b, far_down_b = send_plane(up_b[0], 0, -1), send_plane(down_b[1], 0, 1)
    deltas_b = [line_b[1], up_b[1], far_down_b, down_b[1]]
    partial = roll_back(place, [last(p, weight_in) for p in deltas_b])
    deep = partial[:half] + value(swap(code(partial[half:])))
    deep_four, deep_three, deep_two = code(deep[3 * r :]), code(deep[r : 3 * r]), code(deep[:r])
    from_four = send_z(deep_four, -4)
    from_three = send_z(deep_three, -3)
    others_two = send_z(deep_two, -2)
    from_three = value(lax.optimization_barrier((from_three, from_four, others_two))[0])
    from_one = value(from_one)
    others = swap(code(from_one[r:] + value(others_two) + from_three[r:]))
    grad_x = near[:r] + from_one[:r] + value(from_two) + from_three[:r] + value(from_four) + value(others)

    streams = [tokens_a, tokens_b]
    acts = [line_a[0], up_a[0], far_up_a, down_a[0], line_b[0], up_b[0], far_up_b, down_b[0]]
    deltas += deltas_b
    acts[6], deltas[6] = after((far_up_b, far_down_b), deep)
    inputs, cots = [t[0] for t in streams], [t[1] for t in streams]
    grad_out = grad_kernel(acts, cots, False, factor)
    grad_in = grad_kernel(deltas, inputs, True, factor)
    return (grad_x, grad_in, grad_out)


def solution(mesh):
    in_specs = (P("col", "row"), P("col", "row"), P("row", "col"), P("col", "row"))
    out_specs = (P("col", "row"), P("row", "col"), P("col", "row"))
    return jax.shard_map(
        on_device, mesh=mesh, in_specs=in_specs, out_specs=out_specs, check_vma=False
    )
```

```python
import jax
import jax.numpy as jnp
from jax import lax
from jax.experimental import pallas as pl
from jax.experimental.pallas import tpu as pltpu
from jax.sharding import PartitionSpec as P

root_coef = 0.7978845608028654
cubic_coef = 0.044715
f32, f16, bf16 = jnp.float32, jnp.float16, jnp.bfloat16
AXES = ("row", "col")
SIDE, DEPTH = 4, 8
FF_SCALE, X_SCALE = 1024.0, 32.0
SHORT = pl.CostEstimate(flops=0, transcendentals=0, bytes_accessed=2_000_000)
LONG = pl.CostEstimate(flops=20_000_000_000, transcendentals=0, bytes_accessed=0)


def gelu_parts(preact):
    inner = root_coef * (preact + cubic_coef * preact * preact * preact)
    tanh_value = jnp.tanh(inner)
    activation = 0.5 * preact * (1.0 + tanh_value)
    slopes = 0.5 * (1.0 + tanh_value) + 0.5 * preact * (
        1.0 - tanh_value * tanh_value
    ) * root_coef * (1.0 + 3.0 * cubic_coef * preact * preact)
    return (activation, slopes)


def encode(value, scale):
    size = jnp.abs(value)
    return (value * (lax.rsqrt(jnp.maximum(size, 1e-30)) * scale)).astype(f16)


def decode(code, scale):
    code = code.astype(f32)
    return code * jnp.abs(code) * (1.0 / (scale * scale))


def index(y, x, z, core):
    return ((y % SIDE) * SIDE + x % SIDE) * 2 * DEPTH + (z % DEPTH) * 2 + core


def all_chips():
    return [
        (y, x, z, c)
        for y in range(SIDE)
        for x in range(SIDE)
        for z in range(DEPTH)
        for c in range(2)
    ]


def send_plane(value, axis, step):
    perm = []
    for y, x, z, c in all_chips():
        along_y = (axis == 0) == (c == 0)
        to = (y + step, x) if along_y else (y, x + step)
        perm.append((index(y, x, z, c), index(*to, z, c)))
    return lax.ppermute(value, AXES, perm)


def send_z(value, step):
    perm = [
        (index(y, x, z, c), index(y, x, z + (step if c == 0 else -step), c))
        for y, x, z, c in all_chips()
    ]
    return lax.ppermute(value, AXES, perm)


def swap(value):
    perm = [(index(y, x, z, c), index(y, x, z, 1 - c)) for y, x, z, c in all_chips()]
    return lax.ppermute(value, AXES, perm)


def call(kernel, outs, *operands, scalars=(), **rest):
    specs = [pl.BlockSpec(memory_space=pltpu.SMEM)] * len(scalars)
    specs += [pl.BlockSpec(memory_space=pltpu.VMEM)] * len(operands)
    return pl.pallas_call(
        kernel,
        out_shape=outs,
        in_specs=specs,
        out_specs=pl.BlockSpec(memory_space=pltpu.VMEM),
        compiler_params=pltpu.CompilerParams(vmem_limit_bytes=24 << 20),
        **rest,
    )(*scalars, *operands)


def rolled_block(place, block):
    to_first = lax.rem(block // SIDE + SIDE - place[0], SIDE)
    to_second = lax.rem(block % SIDE + SIDE - place[1], SIDE)
    return to_first * SIDE + to_second


def roll_in(place, pieces, keep, *earlier):
    _, _, n = pieces[0].shape
    total = sum(high - low for low, high in keep)
    size = total // (SIDE * SIDE)

    def kernel(place_ref, *refs):
        out = refs[-1]
        start = 0
        for ref, (low, high) in zip(refs, keep):
            for row in range(low, high, size):
                block = (start + row - low) // size
                to = pl.multiple_of(rolled_block(place_ref, block) * size, size)
                for which in range(2):
                    out[which, pl.ds(to, size), :] = ref[which, row : row + size, :]
            start += high - low

    out = jax.ShapeDtypeStruct((2, total, n), pieces[0].dtype)
    return call(kernel, out, *pieces, *earlier, scalars=(place,), cost_estimate=LONG)


def roll_back(place, pieces, estimate):
    rows, n = pieces[0].shape
    size = rows // SIDE
    total = SIDE * rows

    def kernel(place_ref, *refs):
        out = refs[-1]
        for d, ref in enumerate(refs[:-1]):
            for e in range(SIDE):
                first = lax.rem(place_ref[0] + d, SIDE)
                second = lax.rem(place_ref[1] + e, SIDE)
                to = pl.multiple_of((first * SIDE + second) * size, size)
                out[pl.ds(to, size), :] = ref[e * size : (e + 1) * size, :]

    out = jax.ShapeDtypeStruct((total, n), pieces[0].dtype)
    return call(kernel, out, *pieces, scalars=(place,), cost_estimate=estimate)


def pair_dot(left, right):
    return lax.dot_general(
        left, right, (((2,), (1,)), ((0,), (0,))), preferred_element_type=f32
    )


def tie(*values):
    return lax.optimization_barrier(values)


def first_products(tokens, weights, size):
    return encode(pair_dot(tokens[:, 2 * size : 3 * size], weights), FF_SCALE)


def send_first(far):
    return send_plane(far[:1], 0, 1), send_plane(far[1:], 0, -1)


def second_products(tokens, weights, size, via_up, via_down):
    product = lambda d: pair_dot(tokens[:, d * size : (d + 1) * size], weights)
    via_up, via_down = decode(via_up, FF_SCALE), decode(via_down, FF_SCALE)
    none = jnp.zeros_like(via_up)
    up = encode(product(1) + jnp.concatenate([via_up, none], 0), FF_SCALE)
    down = encode(product(3) + jnp.concatenate([none, via_down], 0), FF_SCALE)
    return up, down


def send_second(up, down):
    return send_plane(up, 0, 1), send_plane(down, 0, -1)


def third_products(tokens, weights, size, from_below, from_above):
    line = pair_dot(tokens[:, :size], weights)
    line = line + decode(from_below, FF_SCALE) + decode(from_above, FF_SCALE)
    rows = size // SIDE
    parts = {d: encode(line[:, d * rows : (d + 1) * rows], FF_SCALE) for d in (2, 1, 3)}
    return line, {d: send_plane(part, 1, d) for d, part in parts.items()}


def hidden_pair(line, parts):
    total = line[:, : line.shape[1] // SIDE]
    for d in (2, 1, 3):
        total = total + decode(parts[d], FF_SCALE)
    activation, slopes = gelu_parts(total[0])
    return jnp.stack([activation.astype(bf16), (total[1] * slopes).astype(bf16)])


def gather_second(own):
    return {d: send_plane(own, 1, -d) for d in (2, 1, 3)}


def gather_first(own, got):
    return jnp.concatenate([own, got[1], got[2], got[3]], 1)


def send_line(line):
    return send_plane(line, 0, -1), send_plane(line, 0, 1)


def last(left, right):
    return lax.dot_general(left, right, (((1,), (1,)), ((), ())), preferred_element_type=f32)


def grad_kernel(pieces, tokens, swapped, factor):
    count = len(pieces)
    rows, hidden = pieces[0].shape
    total, features = count * rows, tokens[0].shape[1]
    tile = hidden // 3

    def kernel(*refs):
        out = refs[-1]
        wide = jnp.concatenate([ref[...] for ref in refs[:count]], 0)
        slim = jnp.concatenate([ref[...] for ref in refs[count:-1]], 0)
        left, right = (slim, wide) if swapped else (wide, slim)
        out[...] = (
            lax.dot_general(left, right, (((0,), (0,)), ((), ())), preferred_element_type=f32)
            * factor
        )

    in_specs = [pl.BlockSpec((rows, tile), lambda i: (0, i))] * count
    in_specs += [pl.BlockSpec(t.shape, lambda i: (0, 0)) for t in tokens]
    if swapped:
        out_spec, out = pl.BlockSpec((features, tile), lambda i: (0, i)), (features, hidden)
    else:
        out_spec, out = pl.BlockSpec((tile, features), lambda i: (i, 0)), (hidden, features)
    return pl.pallas_call(
        kernel,
        grid=(3,),
        in_specs=in_specs,
        out_specs=out_spec,
        out_shape=jax.ShapeDtypeStruct(out, f32),
        compiler_params=pltpu.CompilerParams(vmem_limit_bytes=24 << 20),
        cost_estimate=pl.CostEstimate(
            flops=2 * total * features * hidden,
            transcendentals=0,
            bytes_accessed=2 * total * (features + hidden) + 4 * features * hidden,
        ),
    )(*pieces, *tokens)


def on_device(block_input, cotangent, weight_in, weight_out):
    rows, _ = block_input.shape
    row = lax.axis_index("row")
    core = lax.axis_index("col") % 2
    y, x = row // SIDE, row % SIDE
    place = jnp.where(core == 0, jnp.stack([y, x]), jnp.stack([x, y])).astype(jnp.int32)
    factor = float(rows * 2 * DEPTH) ** (-0.5)
    code = lambda value: encode(value, X_SCALE)
    value = lambda code: decode(code, X_SCALE)

    own = jnp.stack([block_input, cotangent])
    other = swap(own)
    chip = jnp.concatenate([own, other], 1)
    chip, weight_back = tie(chip, weight_out.T)
    weights = jnp.stack([weight_in, weight_back])
    one, two = send_z(chip, 1), send_z(chip, 2)
    other_one, other_two = swap(one), swap(two)
    three, four = send_z(two, 1), send_z(two[:, :rows], 2)
    r = rows
    size = 2 * r
    tokens_a = roll_in(
        place,
        (own, one, two, other, other_one, other_two),
        ((0, r), (0, 2 * r), (0, r)) * 2,
    )
    far_a = first_products(tokens_a, weights, size)
    via_up_a, via_down_a = send_first(far_a)
    mark = far_a[0, :8, :128].astype(f32)
    three, four, mark = tie(three, four, mark)
    other_three, other_four = swap(three), swap(four)
    tokens_b = roll_in(
        place,
        (two, three, four, other_two, other_three, other_four),
        ((r, 2 * r), (0, 2 * r), (0, r)) * 2,
        mark,
    )
    via_up_b, via_down_b = send_first(first_products(tokens_b, weights, size))
    up, down = second_products(tokens_a, weights, size, via_up_a, via_down_a)
    below_a, above_a = send_second(up, down)
    up, down = second_products(tokens_b, weights, size, via_up_b, via_down_b)
    tokens_a, up, down = tie(tokens_a, up, down)
    below_b, above_b = send_second(up, down)
    place_a, parts_a = third_products(tokens_a, weights, size, below_a, above_a)
    pair_a = hidden_pair(place_a, parts_a)
    tokens_b, pair_a = tie(tokens_b, pair_a)
    got_a = gather_second(pair_a)
    place_b, parts_b = third_products(tokens_b, weights, size, below_b, above_b)
    line_a = gather_first(pair_a, got_a)
    place_b, line_a = tie(place_b, line_a)
    up_a, down_a = send_line(line_a)
    pair_b = hidden_pair(place_b, parts_b)
    got_b = gather_second(pair_b)
    pair_b, up_a, down_a = tie(pair_b, up_a, down_a)
    far_up_a, far_down_a = send_plane(up_a[0], 0, -1), send_plane(down_a[1], 0, 1)
    line_b = gather_first(pair_b, got_b)
    up_b, down_b = send_line(line_b)
    far_up_b, far_down_b = send_plane(up_b[0], 0, -1), send_plane(down_b[1], 0, 1)
    far_down_a, up_b, down_b = tie(far_down_a, up_b, down_b)
    deltas = [line_a[1], up_a[1], far_down_a, down_a[1]]
    partial = roll_back(place, [last(p, weight_in) for p in deltas], LONG)
    half = 4 * r
    near = partial[:half] + value(swap(code(partial[half:])))
    near_one, near_two = code(near[r : 3 * r]), code(near[3 * r :])
    from_one, from_two = send_z(near_one, -1), send_z(near_two, -2)
    deltas_b = [line_b[1], up_b[1], far_down_b, down_b[1]]
    partial = roll_back(place, [last(p, weight_in) for p in deltas_b], SHORT)
    deep = partial[:half] + value(swap(code(partial[half:])))
    deep_four, deep_three, deep_two = code(deep[3 * r :]), code(deep[r : 3 * r]), code(deep[:r])
    from_four = send_z(deep_four, -4)
    from_three = send_z(deep_three, -3)
    others_two = send_z(deep_two, -2)
    far_up_a, far_down_a, deep_two = tie(far_up_a, far_down_a, deep_two)
    from_three, from_four, others_two = tie(from_three, from_four, others_two)
    from_one, from_three = value(from_one), value(from_three)
    others = swap(code(from_one[r:] + value(others_two) + from_three[r:]))
    grad_x = near[:r] + from_one[:r] + value(from_two) + from_three[:r] + value(from_four) + value(others)

    streams = [tokens_a, tokens_b]
    inputs, cots = [t[0] for t in streams], [t[1] for t in streams]
    acts = [line_a[0], up_a[0], far_up_a, down_a[0], line_b[0], up_b[0], far_up_b, down_b[0]]
    deltas[2] = far_down_a
    deltas += deltas_b
    grad_out = grad_kernel(acts, cots, False, factor)
    grad_in = grad_kernel(deltas, inputs, True, factor)
    return (grad_x, grad_in, grad_out)


def solution(mesh):
    in_specs = (P("col", "row"), P("col", "row"), P("row", "col"), P("col", "row"))
    out_specs = (P("col", "row"), P("row", "col"), P("col", "row"))
    return jax.shard_map(
        on_device, mesh=mesh, in_specs=in_specs, out_specs=out_specs, check_vma=False
    )
```

```python
import jax
import jax.numpy as jnp
from jax import lax
from jax.experimental import pallas as pl
from jax.experimental.pallas import tpu as pltpu
from jax.sharding import PartitionSpec as P

root_coef = 0.7978845608028654
cubic_coef = 0.044715
f32, f16, bf16 = jnp.float32, jnp.float16, jnp.bfloat16
AXES = ("row", "col")
SIDE, DEPTH = 4, 8
FF_SCALE, X_SCALE = 1024.0, 32.0
SHORT = pl.CostEstimate(flops=0, transcendentals=0, bytes_accessed=2_000_000)
LONG = pl.CostEstimate(flops=20_000_000_000, transcendentals=0, bytes_accessed=0)


def gelu_parts(preact):
    inner = root_coef * (preact + cubic_coef * preact * preact * preact)
    tanh_value = jnp.tanh(inner)
    activation = 0.5 * preact * (1.0 + tanh_value)
    slopes = 0.5 * (1.0 + tanh_value) + 0.5 * preact * (
        1.0 - tanh_value * tanh_value
    ) * root_coef * (1.0 + 3.0 * cubic_coef * preact * preact)
    return (activation, slopes)


def encode(value, scale):
    size = jnp.abs(value)
    return (value * (lax.rsqrt(jnp.maximum(size, 1e-30)) * scale)).astype(f16)


def decode(code, scale):
    code = code.astype(f32)
    return code * jnp.abs(code) * (1.0 / (scale * scale))


def index(y, x, z, core):
    return ((y % SIDE) * SIDE + x % SIDE) * 2 * DEPTH + (z % DEPTH) * 2 + core


def all_chips():
    return [
        (y, x, z, c)
        for y in range(SIDE)
        for x in range(SIDE)
        for z in range(DEPTH)
        for c in range(2)
    ]


def send_plane(value, axis, step):
    perm = []
    for y, x, z, c in all_chips():
        along_y = (axis == 0) == (c == 0)
        to = (y + step, x) if along_y else (y, x + step)
        perm.append((index(y, x, z, c), index(*to, z, c)))
    return lax.ppermute(value, AXES, perm)


def send_z(value, step):
    perm = [
        (index(y, x, z, c), index(y, x, z + (step if c == 0 else -step), c))
        for y, x, z, c in all_chips()
    ]
    return lax.ppermute(value, AXES, perm)


def swap(value):
    perm = [(index(y, x, z, c), index(y, x, z, 1 - c)) for y, x, z, c in all_chips()]
    return lax.ppermute(value, AXES, perm)


def call(kernel, outs, *operands, scalars=(), **rest):
    specs = [pl.BlockSpec(memory_space=pltpu.SMEM)] * len(scalars)
    specs += [pl.BlockSpec(memory_space=pltpu.VMEM)] * len(operands)
    return pl.pallas_call(
        kernel,
        out_shape=outs,
        in_specs=specs,
        out_specs=pl.BlockSpec(memory_space=pltpu.VMEM),
        compiler_params=pltpu.CompilerParams(vmem_limit_bytes=24 << 20),
        **rest,
    )(*scalars, *operands)


def rolled_block(place, block):
    to_first = lax.rem(block // SIDE + SIDE - place[0], SIDE)
    to_second = lax.rem(block % SIDE + SIDE - place[1], SIDE)
    return to_first * SIDE + to_second


def roll_in(place, pieces, keep, *earlier):
    _, _, n = pieces[0].shape
    total = sum(high - low for low, high in keep)
    size = total // (SIDE * SIDE)

    def kernel(place_ref, *refs):
        out = refs[-1]
        start = 0
        for ref, (low, high) in zip(refs, keep):
            for row in range(low, high, size):
                block = (start + row - low) // size
                to = pl.multiple_of(rolled_block(place_ref, block) * size, size)
                for which in range(2):
                    out[which, pl.ds(to, size), :] = ref[which, row : row + size, :]
            start += high - low

    out = jax.ShapeDtypeStruct((2, total, n), pieces[0].dtype)
    return call(kernel, out, *pieces, *earlier, scalars=(place,), cost_estimate=LONG)


def roll_back(place, pieces, estimate):
    rows, n = pieces[0].shape
    size = rows // SIDE
    total = SIDE * rows

    def kernel(place_ref, *refs):
        out = refs[-1]
        for d, ref in enumerate(refs[:-1]):
            for e in range(SIDE):
                first = lax.rem(place_ref[0] + d, SIDE)
                second = lax.rem(place_ref[1] + e, SIDE)
                to = pl.multiple_of((first * SIDE + second) * size, size)
                out[pl.ds(to, size), :] = ref[e * size : (e + 1) * size, :]

    out = jax.ShapeDtypeStruct((total, n), pieces[0].dtype)
    return call(kernel, out, *pieces, scalars=(place,), cost_estimate=estimate)


def pair_dot(left, right):
    return lax.dot_general(
        left, right, (((2,), (1,)), ((0,), (0,))), preferred_element_type=f32
    )


def tie(*values):
    return lax.optimization_barrier(values)


def first_products(tokens, weights, size):
    return encode(pair_dot(tokens[:, 2 * size : 3 * size], weights), FF_SCALE)


def send_first(far):
    return send_plane(far[:1], 0, 1), send_plane(far[1:], 0, -1)


def second_products(tokens, weights, size, via_up, via_down):
    product = lambda d: pair_dot(tokens[:, d * size : (d + 1) * size], weights)
    via_up, via_down = decode(via_up, FF_SCALE), decode(via_down, FF_SCALE)
    none = jnp.zeros_like(via_up)
    up = encode(product(1) + jnp.concatenate([via_up, none], 0), FF_SCALE)
    down = encode(product(3) + jnp.concatenate([none, via_down], 0), FF_SCALE)
    return up, down


def send_second(up, down):
    return send_plane(up, 0, 1), send_plane(down, 0, -1)


def third_products(tokens, weights, size, from_below, from_above):
    line = pair_dot(tokens[:, :size], weights)
    line = line + decode(from_below, FF_SCALE) + decode(from_above, FF_SCALE)
    rows = size // SIDE
    parts = {d: encode(line[:, d * rows : (d + 1) * rows], FF_SCALE) for d in (2, 1, 3)}
    return line, {d: send_plane(part, 1, d) for d, part in parts.items()}


def hidden_pair(line, parts):
    total = line[:, : line.shape[1] // SIDE]
    for d in (2, 1, 3):
        total = total + decode(parts[d], FF_SCALE)
    activation, slopes = gelu_parts(total[0])
    return jnp.stack([activation.astype(bf16), (total[1] * slopes).astype(bf16)])


def gather_second(own):
    return {d: send_plane(own, 1, -d) for d in (2, 1, 3)}


def gather_first(own, got):
    return jnp.concatenate([own, got[1], got[2], got[3]], 1)


def send_line(line):
    return send_plane(line, 0, -1), send_plane(line, 0, 1)


def last(left, right):
    return lax.dot_general(left, right, (((1,), (1,)), ((), ())), preferred_element_type=f32)


def grad_kernel(pieces, tokens, swapped, factor):
    count = len(pieces)
    rows, hidden = pieces[0].shape
    total, features = count * rows, tokens[0].shape[1]
    tile = hidden // 3

    def kernel(*refs):
        out = refs[-1]
        wide = jnp.concatenate([ref[...] for ref in refs[:count]], 0)
        slim = jnp.concatenate([ref[...] for ref in refs[count:-1]], 0)
        left, right = (slim, wide) if swapped else (wide, slim)
        out[...] = (
            lax.dot_general(left, right, (((0,), (0,)), ((), ())), preferred_element_type=f32)
            * factor
        )

    in_specs = [pl.BlockSpec((rows, tile), lambda i: (0, i))] * count
    in_specs += [pl.BlockSpec(t.shape, lambda i: (0, 0)) for t in tokens]
    if swapped:
        out_spec, out = pl.BlockSpec((features, tile), lambda i: (0, i)), (features, hidden)
    else:
        out_spec, out = pl.BlockSpec((tile, features), lambda i: (i, 0)), (hidden, features)
    return pl.pallas_call(
        kernel,
        grid=(3,),
        in_specs=in_specs,
        out_specs=out_spec,
        out_shape=jax.ShapeDtypeStruct(out, f32),
        compiler_params=pltpu.CompilerParams(vmem_limit_bytes=24 << 20),
        cost_estimate=pl.CostEstimate(
            flops=2 * total * features * hidden,
            transcendentals=0,
            bytes_accessed=2 * total * (features + hidden) + 4 * features * hidden,
        ),
    )(*pieces, *tokens)


def on_device(block_input, cotangent, weight_in, weight_out):
    rows, _ = block_input.shape
    row = lax.axis_index("row")
    core = lax.axis_index("col") % 2
    y, x = row // SIDE, row % SIDE
    place = jnp.where(core == 0, jnp.stack([y, x]), jnp.stack([x, y])).astype(jnp.int32)
    factor = float(rows * 2 * DEPTH) ** (-0.5)
    code = lambda value: encode(value, X_SCALE)
    value = lambda code: decode(code, X_SCALE)

    own = jnp.stack([block_input, cotangent])
    other = swap(own)
    chip = jnp.concatenate([own, other], 1)
    chip, weight_back = tie(chip, weight_out.T)
    weights = jnp.stack([weight_in, weight_back])
    one, two = send_z(chip, 1), send_z(chip, 2)
    other_one, other_two = swap(one), swap(two)
    three, four = send_z(two, 1), send_z(two[:, :rows], 2)
    r = rows
    size = 2 * r
    other_three, other_four = swap(three), swap(four)
    tokens_a = roll_in(place, (one, two, other_one, other_two), ((0, 2 * r),) * 4)
    tokens_b = roll_in(
        place,
        (own, three, four, other, other_three, other_four),
        ((0, r), (0, 2 * r), (0, r)) * 2,
    )
    via_up_a, via_down_a = send_first(first_products(tokens_a, weights, size))
    via_up_b, via_down_b = send_first(first_products(tokens_b, weights, size))
    up, down = second_products(tokens_a, weights, size, via_up_a, via_down_a)
    below_a, above_a = send_second(up, down)
    up, down = second_products(tokens_b, weights, size, via_up_b, via_down_b)
    tokens_a, up, down = tie(tokens_a, up, down)
    below_b, above_b = send_second(up, down)
    place_a, parts_a = third_products(tokens_a, weights, size, below_a, above_a)
    pair_a = hidden_pair(place_a, parts_a)
    got_a = gather_second(pair_a)
    place_b, parts_b = third_products(tokens_b, weights, size, below_b, above_b)
    line_a = gather_first(pair_a, got_a)
    place_b, line_a = tie(place_b, line_a)
    up_a, down_a = send_line(line_a)
    pair_b = hidden_pair(place_b, parts_b)
    got_b = gather_second(pair_b)
    pair_b, up_a, down_a = tie(pair_b, up_a, down_a)
    far_up_a, far_down_a = send_plane(up_a[0], 0, -1), send_plane(down_a[1], 0, 1)
    line_b = gather_first(pair_b, got_b)
    up_b, down_b = send_line(line_b)
    far_up_b, far_down_b = send_plane(up_b[0], 0, -1), send_plane(down_b[1], 0, 1)
    far_down_a, up_b, down_b = tie(far_down_a, up_b, down_b)
    deltas = [line_a[1], up_a[1], far_down_a, down_a[1]]
    partial = roll_back(place, [last(p, weight_in) for p in deltas], LONG)
    half = 4 * r
    near = partial[:half] + value(swap(code(partial[half:])))
    from_two = send_z(code(near[2 * r :]), -2)
    from_one = send_z(code(near[: 2 * r]), -1)
    deltas_b = [line_b[1], up_b[1], far_down_b, down_b[1]]
    partial = roll_back(place, [last(p, weight_in) for p in deltas_b], SHORT)
    deep = partial[:half] + value(swap(code(partial[half:])))
    from_four = send_z(code(deep[3 * r :]), -4)
    from_three = send_z(code(deep[r : 3 * r]), -3)
    far_up_a, far_down_a, deep = tie(far_up_a, far_down_a, deep)
    streams = [tokens_a, tokens_b]
    inputs, cots = [t[0] for t in streams], [t[1] for t in streams]
    acts = [line_a[0], up_a[0], far_up_a, down_a[0], line_b[0], up_b[0], far_up_b, down_b[0]]
    deltas[2] = far_down_a
    deltas += deltas_b
    grad_out = grad_kernel(acts, cots, False, factor)
    grad_in = grad_kernel(deltas, inputs, True, factor)
    from_three, from_four, grad_out, grad_in = tie(from_three, from_four, grad_out, grad_in)
    pieces = [value(piece) for piece in (from_one, from_two, from_three)]
    others = value(swap(code(sum(piece[r:] for piece in pieces))))
    grad_x = deep[:r] + value(from_four) + sum(piece[:r] for piece in pieces) + others
    return (grad_x, grad_in, grad_out)


def solution(mesh):
    in_specs = (P("col", "row"), P("col", "row"), P("row", "col"), P("col", "row"))
    out_specs = (P("col", "row"), P("row", "col"), P("col", "row"))
    return jax.shard_map(
        on_device, mesh=mesh, in_specs=in_specs, out_specs=out_specs, check_vma=False
    )
```

```python
import jax
import jax.numpy as jnp
from jax import lax
from jax.experimental import pallas as pl
from jax.experimental.pallas import tpu as pltpu
from jax.sharding import PartitionSpec as P

root_coef = 0.7978845608028654
cubic_coef = 0.044715
f32, f16, bf16 = jnp.float32, jnp.float16, jnp.bfloat16
AXES = ("row", "col")
SIDE, DEPTH = 4, 8
FF_SCALE, X_SCALE = 1024.0, 32.0
SHORT = pl.CostEstimate(flops=0, transcendentals=0, bytes_accessed=2_000_000)
LONG = pl.CostEstimate(flops=20_000_000_000, transcendentals=0, bytes_accessed=0)


def gelu_parts(preact):
    inner = root_coef * (preact + cubic_coef * preact * preact * preact)
    tanh_value = jnp.tanh(inner)
    activation = 0.5 * preact * (1.0 + tanh_value)
    slopes = 0.5 * (1.0 + tanh_value) + 0.5 * preact * (
        1.0 - tanh_value * tanh_value
    ) * root_coef * (1.0 + 3.0 * cubic_coef * preact * preact)
    return (activation, slopes)


def encode(value, scale):
    size = jnp.abs(value)
    return (value * (lax.rsqrt(jnp.maximum(size, 1e-30)) * scale)).astype(f16)


def decode(code, scale):
    code = code.astype(f32)
    return code * jnp.abs(code) * (1.0 / (scale * scale))


def index(y, x, z, core):
    return ((y % SIDE) * SIDE + x % SIDE) * 2 * DEPTH + (z % DEPTH) * 2 + core


def all_chips():
    return [
        (y, x, z, c)
        for y in range(SIDE)
        for x in range(SIDE)
        for z in range(DEPTH)
        for c in range(2)
    ]


def send_plane(value, axis, step):
    perm = []
    for y, x, z, c in all_chips():
        along_y = (axis == 0) == (c == 0)
        to = (y + step, x) if along_y else (y, x + step)
        perm.append((index(y, x, z, c), index(*to, z, c)))
    return lax.ppermute(value, AXES, perm)


def send_z(value, step):
    perm = [
        (index(y, x, z, c), index(y, x, z + (step if c == 0 else -step), c))
        for y, x, z, c in all_chips()
    ]
    return lax.ppermute(value, AXES, perm)


def swap(value):
    perm = [(index(y, x, z, c), index(y, x, z, 1 - c)) for y, x, z, c in all_chips()]
    return lax.ppermute(value, AXES, perm)


def call(kernel, outs, *operands, scalars=(), **rest):
    specs = [pl.BlockSpec(memory_space=pltpu.SMEM)] * len(scalars)
    specs += [pl.BlockSpec(memory_space=pltpu.VMEM)] * len(operands)
    return pl.pallas_call(
        kernel,
        out_shape=outs,
        in_specs=specs,
        out_specs=pl.BlockSpec(memory_space=pltpu.VMEM),
        compiler_params=pltpu.CompilerParams(vmem_limit_bytes=24 << 20),
        **rest,
    )(*scalars, *operands)


def rolled_block(place, block):
    to_first = lax.rem(block // SIDE + SIDE - place[0], SIDE)
    to_second = lax.rem(block % SIDE + SIDE - place[1], SIDE)
    return to_first * SIDE + to_second


def roll_in(place, pieces, keep, *earlier):
    _, _, n = pieces[0].shape
    total = sum(high - low for low, high in keep)
    size = total // (SIDE * SIDE)

    def kernel(place_ref, *refs):
        out = refs[-1]
        start = 0
        for ref, (low, high) in zip(refs, keep):
            for row in range(low, high, size):
                block = (start + row - low) // size
                to = pl.multiple_of(rolled_block(place_ref, block) * size, size)
                for which in range(2):
                    out[which, pl.ds(to, size), :] = ref[which, row : row + size, :]
            start += high - low

    out = jax.ShapeDtypeStruct((2, total, n), pieces[0].dtype)
    return call(kernel, out, *pieces, *earlier, scalars=(place,), cost_estimate=LONG)


def roll_back(place, pieces, estimate):
    rows, n = pieces[0].shape
    size = rows // SIDE
    total = SIDE * rows

    def kernel(place_ref, *refs):
        out = refs[-1]
        for d, ref in enumerate(refs[:-1]):
            for e in range(SIDE):
                first = lax.rem(place_ref[0] + d, SIDE)
                second = lax.rem(place_ref[1] + e, SIDE)
                to = pl.multiple_of((first * SIDE + second) * size, size)
                out[pl.ds(to, size), :] = ref[e * size : (e + 1) * size, :]

    out = jax.ShapeDtypeStruct((total, n), pieces[0].dtype)
    return call(kernel, out, *pieces, scalars=(place,), cost_estimate=estimate)


def pair_dot(left, right):
    return lax.dot_general(
        left, right, (((2,), (1,)), ((0,), (0,))), preferred_element_type=f32
    )


def tie(*values):
    return lax.optimization_barrier(values)


def first_products(tokens, weights, size):
    return encode(pair_dot(tokens[:, 2 * size : 3 * size], weights), FF_SCALE)


def send_first(far):
    return send_plane(far[:1], 0, 1), send_plane(far[1:], 0, -1)


def second_products(tokens, weights, size, via_up, via_down):
    product = lambda d: pair_dot(tokens[:, d * size : (d + 1) * size], weights)
    via_up, via_down = decode(via_up, FF_SCALE), decode(via_down, FF_SCALE)
    none = jnp.zeros_like(via_up)
    up = encode(product(1) + jnp.concatenate([via_up, none], 0), FF_SCALE)
    down = encode(product(3) + jnp.concatenate([none, via_down], 0), FF_SCALE)
    return up, down


def send_second(up, down):
    return send_plane(up, 0, 1), send_plane(down, 0, -1)


def third_products(tokens, weights, size, from_below, from_above):
    line = pair_dot(tokens[:, :size], weights)
    line = line + decode(from_below, FF_SCALE) + decode(from_above, FF_SCALE)
    rows = size // SIDE
    parts = {d: encode(line[:, d * rows : (d + 1) * rows], FF_SCALE) for d in (2, 1, 3)}
    return line, {d: send_plane(part, 1, d) for d, part in parts.items()}


def hidden_pair(line, parts):
    total = line[:, : line.shape[1] // SIDE]
    for d in (2, 1, 3):
        total = total + decode(parts[d], FF_SCALE)
    activation, slopes = gelu_parts(total[0])
    return jnp.stack([activation.astype(bf16), (total[1] * slopes).astype(bf16)])


def gather_second(own):
    return {d: send_plane(own, 1, -d) for d in (2, 1, 3)}


def gather_first(own, got):
    return jnp.concatenate([own, got[1], got[2], got[3]], 1)


def send_line(line):
    return send_plane(line, 0, -1), send_plane(line, 0, 1)


def last(left, right):
    return lax.dot_general(left, right, (((1,), (1,)), ((), ())), preferred_element_type=f32)


def grad_kernel(pieces, tokens, swapped, factor):
    count = len(pieces)
    rows, hidden = pieces[0].shape
    total, features = count * rows, tokens[0].shape[1]
    tile = hidden // 3

    def kernel(*refs):
        out = refs[-1]
        wide = jnp.concatenate([ref[...] for ref in refs[:count]], 0)
        slim = jnp.concatenate([ref[...] for ref in refs[count:-1]], 0)
        left, right = (slim, wide) if swapped else (wide, slim)
        out[...] = (
            lax.dot_general(left, right, (((0,), (0,)), ((), ())), preferred_element_type=f32)
            * factor
        )

    in_specs = [pl.BlockSpec((rows, tile), lambda i: (0, i))] * count
    in_specs += [pl.BlockSpec(t.shape, lambda i: (0, 0)) for t in tokens]
    if swapped:
        out_spec, out = pl.BlockSpec((features, tile), lambda i: (0, i)), (features, hidden)
    else:
        out_spec, out = pl.BlockSpec((tile, features), lambda i: (i, 0)), (hidden, features)
    return pl.pallas_call(
        kernel,
        grid=(3,),
        in_specs=in_specs,
        out_specs=out_spec,
        out_shape=jax.ShapeDtypeStruct(out, f32),
        compiler_params=pltpu.CompilerParams(vmem_limit_bytes=24 << 20),
        cost_estimate=pl.CostEstimate(
            flops=2 * total * features * hidden,
            transcendentals=0,
            bytes_accessed=2 * total * (features + hidden) + 4 * features * hidden,
        ),
    )(*pieces, *tokens)


def on_device(block_input, cotangent, weight_in, weight_out):
    rows, _ = block_input.shape
    row = lax.axis_index("row")
    core = lax.axis_index("col") % 2
    y, x = row // SIDE, row % SIDE
    place = jnp.where(core == 0, jnp.stack([y, x]), jnp.stack([x, y])).astype(jnp.int32)
    factor = float(rows * 2 * DEPTH) ** (-0.5)
    code = lambda value: encode(value, X_SCALE)
    value = lambda code: decode(code, X_SCALE)

    own = jnp.stack([block_input, cotangent])
    other = swap(own)
    chip = jnp.concatenate([own, other], 1)
    chip, weight_back = tie(chip, weight_out.T)
    weights = jnp.stack([weight_in, weight_back])
    one, two = send_z(chip, 1), send_z(chip, 2)
    other_one, other_two = swap(one), swap(two)
    three, four = send_z(two, 1), send_z(two[:, :rows], 2)
    r = rows
    size = 2 * r
    other_three, other_four = swap(three), swap(four)
    tokens_a = roll_in(place, (one, two, other_one, other_two), ((0, 2 * r),) * 4)
    tokens_b = roll_in(
        place,
        (own, three, four, other, other_three, other_four),
        ((0, r), (0, 2 * r), (0, r)) * 2,
    )
    via_up_a, via_down_a = send_first(first_products(tokens_a, weights, size))
    via_up_b, via_down_b = send_first(first_products(tokens_b, weights, size))
    up, down = second_products(tokens_a, weights, size, via_up_a, via_down_a)
    below_a, above_a = send_second(up, down)
    up, down = second_products(tokens_b, weights, size, via_up_b, via_down_b)
    tokens_a, up, down = tie(tokens_a, up, down)
    below_b, above_b = send_second(up, down)
    place_a, parts_a = third_products(tokens_a, weights, size, below_a, above_a)
    pair_a = hidden_pair(place_a, parts_a)
    got_a = gather_second(pair_a)
    place_b, parts_b = third_products(tokens_b, weights, size, below_b, above_b)
    line_a = gather_first(pair_a, got_a)
    place_b, line_a = tie(place_b, line_a)
    up_a, down_a = send_line(line_a)
    pair_b = hidden_pair(place_b, parts_b)
    got_b = gather_second(pair_b)
    pair_b, up_a, down_a = tie(pair_b, up_a, down_a)
    far_up_a, far_down_a = send_plane(up_a[0], 0, -1), send_plane(down_a[1], 0, 1)
    line_b = gather_first(pair_b, got_b)
    up_b, down_b = send_line(line_b)
    far_up_b, far_down_b = send_plane(up_b[0], 0, -1), send_plane(down_b[1], 0, 1)
    far_down_a, up_b, down_b = tie(far_down_a, up_b, down_b)
    deltas = [line_a[1], up_a[1], far_down_a, down_a[1]]
    partial = roll_back(place, [last(p, weight_in) for p in deltas], LONG)
    half = 4 * r
    near = partial[:half] + value(swap(code(partial[half:])))
    from_two = send_z(code(near[2 * r :]), -2)
    from_one = send_z(code(near[: 2 * r]), -1)
    deltas_b = [line_b[1], up_b[1], far_down_b, down_b[1]]
    partial = roll_back(place, [last(p, weight_in) for p in deltas_b], SHORT)
    deep = partial[:half] + value(swap(code(partial[half:])))
    from_four = send_z(code(deep[3 * r :]), -4)
    from_three = send_z(code(deep[r : 3 * r]), -3)
    far_up_a, far_down_a, deep = tie(far_up_a, far_down_a, deep)
    streams = [tokens_a, tokens_b]
    inputs, cots = [t[0] for t in streams], [t[1] for t in streams]
    acts = [line_a[0], up_a[0], far_up_a, down_a[0], line_b[0], up_b[0], far_up_b, down_b[0]]
    deltas[2] = far_down_a
    deltas += deltas_b
    grad_out = grad_kernel(acts, cots, False, factor)
    grad_in = grad_kernel(deltas, inputs, True, factor)
    from_one, from_two, from_three, from_four, grad_out, grad_in = tie(
        from_one, from_two, from_three, from_four, grad_out, grad_in
    )
    pieces = [value(piece) for piece in (from_one, from_two, from_three)]
    others = value(swap(code(sum(piece[r:] for piece in pieces))))
    grad_x = deep[:r] + value(from_four) + sum(piece[:r] for piece in pieces) + others
    return (grad_x, grad_in, grad_out)


def solution(mesh):
    in_specs = (P("col", "row"), P("col", "row"), P("row", "col"), P("col", "row"))
    out_specs = (P("col", "row"), P("row", "col"), P("col", "row"))
    return jax.shard_map(
        on_device, mesh=mesh, in_specs=in_specs, out_specs=out_specs, check_vma=False
    )
```

```python
import jax
import jax.numpy as jnp
from jax import lax
from jax.experimental import pallas as pl
from jax.experimental.pallas import tpu as pltpu
from jax.sharding import PartitionSpec as P

root_coef = 0.7978845608028654
cubic_coef = 0.044715
f32, f16, bf16 = jnp.float32, jnp.float16, jnp.bfloat16
AXES = ("row", "col")
SIDE, DEPTH = 4, 8
FF_SCALE, X_SCALE = 1024.0, 32.0
SHORT = pl.CostEstimate(flops=0, transcendentals=0, bytes_accessed=2_000_000)
LONG = pl.CostEstimate(flops=20_000_000_000, transcendentals=0, bytes_accessed=0)


def gelu_parts(preact):
    inner = root_coef * (preact + cubic_coef * preact * preact * preact)
    tanh_value = jnp.tanh(inner)
    activation = 0.5 * preact * (1.0 + tanh_value)
    slopes = 0.5 * (1.0 + tanh_value) + 0.5 * preact * (
        1.0 - tanh_value * tanh_value
    ) * root_coef * (1.0 + 3.0 * cubic_coef * preact * preact)
    return (activation, slopes)


def encode(value, scale):
    size = jnp.abs(value)
    return (value * (lax.rsqrt(jnp.maximum(size, 1e-30)) * scale)).astype(f16)


def decode(code, scale):
    code = code.astype(f32)
    return code * jnp.abs(code) * (1.0 / (scale * scale))


def index(y, x, z, core):
    return ((y % SIDE) * SIDE + x % SIDE) * 2 * DEPTH + (z % DEPTH) * 2 + core


def all_chips():
    return [
        (y, x, z, c)
        for y in range(SIDE)
        for x in range(SIDE)
        for z in range(DEPTH)
        for c in range(2)
    ]


def send_plane(value, axis, step):
    perm = []
    for y, x, z, c in all_chips():
        along_y = (axis == 0) == (c == 0)
        to = (y + step, x) if along_y else (y, x + step)
        perm.append((index(y, x, z, c), index(*to, z, c)))
    return lax.ppermute(value, AXES, perm)


def send_z(value, step):
    perm = [
        (index(y, x, z, c), index(y, x, z + (step if c == 0 else -step), c))
        for y, x, z, c in all_chips()
    ]
    return lax.ppermute(value, AXES, perm)


def swap(value):
    perm = [(index(y, x, z, c), index(y, x, z, 1 - c)) for y, x, z, c in all_chips()]
    return lax.ppermute(value, AXES, perm)


def call(kernel, outs, *operands, scalars=(), **rest):
    specs = [pl.BlockSpec(memory_space=pltpu.SMEM)] * len(scalars)
    specs += [pl.BlockSpec(memory_space=pltpu.VMEM)] * len(operands)
    return pl.pallas_call(
        kernel,
        out_shape=outs,
        in_specs=specs,
        out_specs=pl.BlockSpec(memory_space=pltpu.VMEM),
        compiler_params=pltpu.CompilerParams(vmem_limit_bytes=24 << 20),
        **rest,
    )(*scalars, *operands)


def rolled_block(place, block):
    to_first = lax.rem(block // SIDE + SIDE - place[0], SIDE)
    to_second = lax.rem(block % SIDE + SIDE - place[1], SIDE)
    return to_first * SIDE + to_second


def roll_in(place, pieces, keep, *earlier):
    _, _, n = pieces[0].shape
    total = sum(high - low for low, high in keep)
    size = total // (SIDE * SIDE)

    def kernel(place_ref, *refs):
        out = refs[-1]
        start = 0
        for ref, (low, high) in zip(refs, keep):
            for row in range(low, high, size):
                block = (start + row - low) // size
                to = pl.multiple_of(rolled_block(place_ref, block) * size, size)
                for which in range(2):
                    out[which, pl.ds(to, size), :] = ref[which, row : row + size, :]
            start += high - low

    out = jax.ShapeDtypeStruct((2, total, n), pieces[0].dtype)
    return call(kernel, out, *pieces, *earlier, scalars=(place,), cost_estimate=LONG)


def roll_back(place, pieces, estimate):
    rows, n = pieces[0].shape
    size = rows // SIDE
    total = SIDE * rows

    def kernel(place_ref, *refs):
        out = refs[-1]
        for d, ref in enumerate(refs[:-1]):
            for e in range(SIDE):
                first = lax.rem(place_ref[0] + d, SIDE)
                second = lax.rem(place_ref[1] + e, SIDE)
                to = pl.multiple_of((first * SIDE + second) * size, size)
                out[pl.ds(to, size), :] = ref[e * size : (e + 1) * size, :]

    out = jax.ShapeDtypeStruct((total, n), pieces[0].dtype)
    return call(kernel, out, *pieces, scalars=(place,), cost_estimate=estimate)


def pair_dot(left, right):
    return lax.dot_general(
        left, right, (((2,), (1,)), ((0,), (0,))), preferred_element_type=f32
    )


def tie(*values):
    return lax.optimization_barrier(values)


def first_products(tokens, weights, size):
    return encode(pair_dot(tokens[:, 2 * size : 3 * size], weights), FF_SCALE)


def send_first(far):
    return send_plane(far[:1], 0, 1), send_plane(far[1:], 0, -1)


def second_products(tokens, weights, size, via_up, via_down):
    product = lambda d: pair_dot(tokens[:, d * size : (d + 1) * size], weights)
    via_up, via_down = decode(via_up, FF_SCALE), decode(via_down, FF_SCALE)
    none = jnp.zeros_like(via_up)
    up = encode(product(1) + jnp.concatenate([via_up, none], 0), FF_SCALE)
    down = encode(product(3) + jnp.concatenate([none, via_down], 0), FF_SCALE)
    return up, down


def send_second(up, down):
    return send_plane(up, 0, 1), send_plane(down, 0, -1)


def third_products(tokens, weights, size, from_below, from_above):
    line = pair_dot(tokens[:, :size], weights)
    line = line + decode(from_below, FF_SCALE) + decode(from_above, FF_SCALE)
    rows = size // SIDE
    parts = {d: encode(line[:, d * rows : (d + 1) * rows], FF_SCALE) for d in (2, 1, 3)}
    return line, {d: send_plane(part, 1, d) for d, part in parts.items()}


def hidden_pair(line, parts):
    total = line[:, : line.shape[1] // SIDE]
    for d in (2, 1, 3):
        total = total + decode(parts[d], FF_SCALE)
    activation, slopes = gelu_parts(total[0])
    return jnp.stack([activation.astype(bf16), (total[1] * slopes).astype(bf16)])


def gather_second(own):
    return {d: send_plane(own, 1, -d) for d in (2, 1, 3)}


def gather_first(own, got):
    return jnp.concatenate([own, got[1], got[2], got[3]], 1)


def send_line(line):
    return send_plane(line, 0, -1), send_plane(line, 0, 1)


def last(left, right):
    return lax.dot_general(left, right, (((1,), (1,)), ((), ())), preferred_element_type=f32)


def grad_kernel(pieces, tokens, swapped, factor):
    count = len(pieces)
    rows, hidden = pieces[0].shape
    total, features = count * rows, tokens[0].shape[1]
    tile = hidden // 2

    def kernel(*refs):
        out = refs[-1]
        wide = jnp.concatenate([ref[...] for ref in refs[:count]], 0)
        slim = jnp.concatenate([ref[...] for ref in refs[count:-1]], 0)
        left, right = (slim, wide) if swapped else (wide, slim)
        out[...] = (
            lax.dot_general(left, right, (((0,), (0,)), ((), ())), preferred_element_type=f32)
            * factor
        )

    in_specs = [pl.BlockSpec((rows, tile), lambda i: (0, i))] * count
    in_specs += [pl.BlockSpec(t.shape, lambda i: (0, 0)) for t in tokens]
    if swapped:
        out_spec, out = pl.BlockSpec((features, tile), lambda i: (0, i)), (features, hidden)
    else:
        out_spec, out = pl.BlockSpec((tile, features), lambda i: (i, 0)), (hidden, features)
    return pl.pallas_call(
        kernel,
        grid=(2,),
        in_specs=in_specs,
        out_specs=out_spec,
        out_shape=jax.ShapeDtypeStruct(out, f32),
        compiler_params=pltpu.CompilerParams(vmem_limit_bytes=24 << 20),
        cost_estimate=pl.CostEstimate(
            flops=2 * total * features * hidden,
            transcendentals=0,
            bytes_accessed=2 * total * (features + hidden) + 4 * features * hidden,
        ),
    )(*pieces, *tokens)


def on_device(block_input, cotangent, weight_in, weight_out):
    rows, _ = block_input.shape
    row = lax.axis_index("row")
    core = lax.axis_index("col") % 2
    y, x = row // SIDE, row % SIDE
    place = jnp.where(core == 0, jnp.stack([y, x]), jnp.stack([x, y])).astype(jnp.int32)
    factor = float(rows * 2 * DEPTH) ** (-0.5)
    code = lambda value: encode(value, X_SCALE)
    value = lambda code: decode(code, X_SCALE)

    own = jnp.stack([block_input, cotangent])
    other = swap(own)
    chip = jnp.concatenate([own, other], 1)
    two = send_z(chip, 2)
    chip, weight_back = tie(chip, weight_out.T)
    weights = jnp.stack([weight_in, weight_back])
    one = send_z(chip, 1)
    three, four = send_z(two, 1), send_z(two[:, :rows], 2)
    other_one, other_two = swap(one), swap(two)
    r = rows
    size = 2 * r
    other_three, other_four = swap(three), swap(four)
    tokens_a = roll_in(place, (one, two, other_one, other_two), ((0, 2 * r),) * 4)
    tokens_b = roll_in(
        place,
        (own, three, four, other, other_three, other_four),
        ((0, r), (0, 2 * r), (0, r)) * 2,
    )
    via_up_a, via_down_a = send_first(first_products(tokens_a, weights, size))
    via_up_b, via_down_b = send_first(first_products(tokens_b, weights, size))
    up, down = second_products(tokens_a, weights, size, via_up_a, via_down_a)
    below_a, above_a = send_second(up, down)
    up, down = second_products(tokens_b, weights, size, via_up_b, via_down_b)
    tokens_a, up, down = tie(tokens_a, up, down)
    below_b, above_b = send_second(up, down)
    place_a, parts_a = third_products(tokens_a, weights, size, below_a, above_a)
    pair_a = hidden_pair(place_a, parts_a)
    got_a = gather_second(pair_a)
    place_b, parts_b = third_products(tokens_b, weights, size, below_b, above_b)
    line_a = gather_first(pair_a, got_a)
    place_b, line_a = tie(place_b, line_a)
    up_a, down_a = send_line(line_a)
    pair_b = hidden_pair(place_b, parts_b)
    got_b = gather_second(pair_b)
    pair_b, up_a, down_a = tie(pair_b, up_a, down_a)
    far_up_a, far_down_a = send_plane(up_a[0], 0, -1), send_plane(down_a[1], 0, 1)
    line_b = gather_first(pair_b, got_b)
    up_b, down_b = send_line(line_b)
    far_up_b, far_down_b = send_plane(up_b[0], 0, -1), send_plane(down_b[1], 0, 1)
    far_down_a, up_b, down_b = tie(far_down_a, up_b, down_b)
    deltas = [line_a[1], up_a[1], far_down_a, down_a[1]]
    partial = roll_back(place, [last(p, weight_in) for p in deltas], LONG)
    half = 4 * r
    near = partial[:half] + value(swap(code(partial[half:])))
    from_two = send_z(code(near[2 * r :]), -2)
    from_one = send_z(code(near[: 2 * r]), -1)
    deltas_b = [line_b[1], up_b[1], far_down_b, down_b[1]]
    partial = roll_back(place, [last(p, weight_in) for p in deltas_b], SHORT)
    deep = partial[:half] + value(swap(code(partial[half:])))
    from_four = send_z(code(deep[3 * r :]), -4)
    from_three = send_z(code(deep[r : 3 * r]), -3)
    far_up_a, far_down_a, deep = tie(far_up_a, far_down_a, deep)
    streams = [tokens_a, tokens_b]
    inputs, cots = [t[0] for t in streams], [t[1] for t in streams]
    acts = [line_a[0], up_a[0], far_up_a, down_a[0], line_b[0], up_b[0], far_up_b, down_b[0]]
    deltas[2] = far_down_a
    deltas += deltas_b
    grad_out = grad_kernel(acts, cots, False, factor)
    grad_in = grad_kernel(deltas, inputs, True, factor)
    from_one, from_two, from_three, from_four, grad_out, grad_in = tie(
        from_one, from_two, from_three, from_four, grad_out, grad_in
    )
    pieces = [value(piece) for piece in (from_one, from_two, from_three)]
    others = value(swap(code(sum(piece[r:] for piece in pieces))))
    grad_x = deep[:r] + value(from_four) + sum(piece[:r] for piece in pieces) + others
    return (grad_x, grad_in, grad_out)


def solution(mesh):
    in_specs = (P("col", "row"), P("col", "row"), P("row", "col"), P("col", "row"))
    out_specs = (P("col", "row"), P("row", "col"), P("col", "row"))
    return jax.shard_map(
        on_device, mesh=mesh, in_specs=in_specs, out_specs=out_specs, check_vma=False
    )
```

```python
import jax
import jax.numpy as jnp
from jax import lax
from jax.experimental import pallas as pl
from jax.experimental.pallas import tpu as pltpu
from jax.sharding import PartitionSpec as P

root_coef = 0.7978845608028654
cubic_coef = 0.044715
f32, f16, bf16 = jnp.float32, jnp.float16, jnp.bfloat16
AXES = ("row", "col")
SIDE, DEPTH = 4, 8
FF_SCALE, X_SCALE = 1024.0, 32.0
SHORT = pl.CostEstimate(flops=0, transcendentals=0, bytes_accessed=2_000_000)
LONG = pl.CostEstimate(flops=20_000_000_000, transcendentals=0, bytes_accessed=0)


def gelu_parts(preact):
    inner = root_coef * (preact + cubic_coef * preact * preact * preact)
    tanh_value = jnp.tanh(inner)
    activation = 0.5 * preact * (1.0 + tanh_value)
    slopes = 0.5 * (1.0 + tanh_value) + 0.5 * preact * (
        1.0 - tanh_value * tanh_value
    ) * root_coef * (1.0 + 3.0 * cubic_coef * preact * preact)
    return (activation, slopes)


def encode(value, scale):
    size = jnp.abs(value)
    return (value * (lax.rsqrt(jnp.maximum(size, 1e-30)) * scale)).astype(f16)


def decode(code, scale):
    code = code.astype(f32)
    return code * jnp.abs(code) * (1.0 / (scale * scale))


def index(y, x, z, core):
    return ((y % SIDE) * SIDE + x % SIDE) * 2 * DEPTH + (z % DEPTH) * 2 + core


def all_chips():
    return [
        (y, x, z, c)
        for y in range(SIDE)
        for x in range(SIDE)
        for z in range(DEPTH)
        for c in range(2)
    ]


def send_plane(value, axis, step):
    perm = []
    for y, x, z, c in all_chips():
        along_y = (axis == 0) == (c == 0)
        to = (y + step, x) if along_y else (y, x + step)
        perm.append((index(y, x, z, c), index(*to, z, c)))
    return lax.ppermute(value, AXES, perm)


def send_z(value, step):
    perm = [
        (index(y, x, z, c), index(y, x, z + (step if c == 0 else -step), c))
        for y, x, z, c in all_chips()
    ]
    return lax.ppermute(value, AXES, perm)


def swap(value):
    perm = [(index(y, x, z, c), index(y, x, z, 1 - c)) for y, x, z, c in all_chips()]
    return lax.ppermute(value, AXES, perm)


def call(kernel, outs, *operands, scalars=(), **rest):
    specs = [pl.BlockSpec(memory_space=pltpu.SMEM)] * len(scalars)
    specs += [pl.BlockSpec(memory_space=pltpu.VMEM)] * len(operands)
    return pl.pallas_call(
        kernel,
        out_shape=outs,
        in_specs=specs,
        out_specs=pl.BlockSpec(memory_space=pltpu.VMEM),
        compiler_params=pltpu.CompilerParams(vmem_limit_bytes=24 << 20),
        **rest,
    )(*scalars, *operands)


def rolled_block(place, block):
    to_first = lax.rem(block // SIDE + SIDE - place[0], SIDE)
    to_second = lax.rem(block % SIDE + SIDE - place[1], SIDE)
    return to_first * SIDE + to_second


def roll_in(place, pieces, keep, *earlier):
    _, _, n = pieces[0].shape
    total = sum(high - low for low, high in keep)
    size = total // (SIDE * SIDE)

    def kernel(place_ref, *refs):
        out = refs[-1]
        start = 0
        for ref, (low, high) in zip(refs, keep):
            for row in range(low, high, size):
                block = (start + row - low) // size
                to = pl.multiple_of(rolled_block(place_ref, block) * size, size)
                for which in range(2):
                    out[which, pl.ds(to, size), :] = ref[which, row : row + size, :]
            start += high - low

    out = jax.ShapeDtypeStruct((2, total, n), pieces[0].dtype)
    return call(kernel, out, *pieces, *earlier, scalars=(place,), cost_estimate=LONG)


def roll_back(place, pieces, estimate):
    rows, n = pieces[0].shape
    size = rows // SIDE
    total = SIDE * rows

    def kernel(place_ref, *refs):
        out = refs[-1]
        for d, ref in enumerate(refs[:-1]):
            for e in range(SIDE):
                first = lax.rem(place_ref[0] + d, SIDE)
                second = lax.rem(place_ref[1] + e, SIDE)
                to = pl.multiple_of((first * SIDE + second) * size, size)
                out[pl.ds(to, size), :] = ref[e * size : (e + 1) * size, :]

    out = jax.ShapeDtypeStruct((total, n), pieces[0].dtype)
    return call(kernel, out, *pieces, scalars=(place,), cost_estimate=estimate)


def pair_dot(left, right):
    return lax.dot_general(
        left, right, (((2,), (1,)), ((0,), (0,))), preferred_element_type=f32
    )


def tie(*values):
    return lax.optimization_barrier(values)


def first_products(tokens, weights, size):
    return encode(pair_dot(tokens[:, 2 * size : 3 * size], weights), FF_SCALE)


def send_first(far):
    return send_plane(far[:1], 0, 1), send_plane(far[1:], 0, -1)


def second_products(tokens, weights, size, via_up, via_down):
    product = lambda d: pair_dot(tokens[:, d * size : (d + 1) * size], weights)
    via_up, via_down = decode(via_up, FF_SCALE), decode(via_down, FF_SCALE)
    none = jnp.zeros_like(via_up)
    up = encode(product(1) + jnp.concatenate([via_up, none], 0), FF_SCALE)
    down = encode(product(3) + jnp.concatenate([none, via_down], 0), FF_SCALE)
    return up, down


def send_second(up, down):
    return send_plane(up, 0, 1), send_plane(down, 0, -1)


def third_products(tokens, weights, size, from_below, from_above):
    line = pair_dot(tokens[:, :size], weights)
    line = line + decode(from_below, FF_SCALE) + decode(from_above, FF_SCALE)
    rows = size // SIDE
    parts = {d: encode(line[:, d * rows : (d + 1) * rows], FF_SCALE) for d in (2, 1, 3)}
    return line, {d: send_plane(part, 1, d) for d, part in parts.items()}


def hidden_pair(line, parts):
    total = line[:, : line.shape[1] // SIDE]
    for d in (2, 1, 3):
        total = total + decode(parts[d], FF_SCALE)
    activation, slopes = gelu_parts(total[0])
    return jnp.stack([activation.astype(bf16), (total[1] * slopes).astype(bf16)])


def gather_second(own):
    return {d: send_plane(own, 1, -d) for d in (2, 1, 3)}


def gather_first(own, got):
    return jnp.concatenate([own, got[1], got[2], got[3]], 1)


def send_line(line):
    return send_plane(line, 0, -1), send_plane(line, 0, 1)


def last(left, right):
    return lax.dot_general(left, right, (((1,), (1,)), ((), ())), preferred_element_type=f32)


def grad_kernel(pieces, tokens, swapped, factor):
    count = len(pieces)
    rows, hidden = pieces[0].shape
    total, features = count * rows, tokens[0].shape[1]
    tile = hidden // 2

    def kernel(*refs):
        out = refs[-1]
        wide = jnp.concatenate([ref[...] for ref in refs[:count]], 0)
        slim = jnp.concatenate([ref[...] for ref in refs[count:-1]], 0)
        left, right = (slim, wide) if swapped else (wide, slim)
        out[...] = (
            lax.dot_general(left, right, (((0,), (0,)), ((), ())), preferred_element_type=f32)
            * factor
        )

    in_specs = [pl.BlockSpec((rows, tile), lambda i: (0, i))] * count
    in_specs += [pl.BlockSpec(t.shape, lambda i: (0, 0)) for t in tokens]
    if swapped:
        out_spec, out = pl.BlockSpec((features, tile), lambda i: (0, i)), (features, hidden)
    else:
        out_spec, out = pl.BlockSpec((tile, features), lambda i: (i, 0)), (hidden, features)
    return pl.pallas_call(
        kernel,
        grid=(2,),
        in_specs=in_specs,
        out_specs=out_spec,
        out_shape=jax.ShapeDtypeStruct(out, f32),
        compiler_params=pltpu.CompilerParams(vmem_limit_bytes=24 << 20),
        cost_estimate=pl.CostEstimate(
            flops=2 * total * features * hidden,
            transcendentals=0,
            bytes_accessed=2 * total * (features + hidden) + 4 * features * hidden,
        ),
    )(*pieces, *tokens)


def on_device(block_input, cotangent, weight_in, weight_out):
    rows, _ = block_input.shape
    row = lax.axis_index("row")
    core = lax.axis_index("col") % 2
    y, x = row // SIDE, row % SIDE
    place = jnp.where(core == 0, jnp.stack([y, x]), jnp.stack([x, y])).astype(jnp.int32)
    factor = float(rows * 2 * DEPTH) ** (-0.5)
    code = lambda value: encode(value, X_SCALE)
    value = lambda code: decode(code, X_SCALE)

    own = jnp.stack([block_input, cotangent])
    other = swap(own)
    chip = jnp.concatenate([own, other], 1)
    two = send_z(chip, 2)
    chip, weight_back = tie(chip, weight_out.T)
    weights = jnp.stack([weight_in, weight_back])
    one = send_z(chip, 1)
    three, four = send_z(two, 1), send_z(two[:, :rows], 2)
    other_one, other_two = swap(one), swap(two)
    r = rows
    size = 2 * r
    other_three, other_four = swap(three), swap(four)
    tokens_a = roll_in(place, (one, two, other_one, other_two), ((0, 2 * r),) * 4)
    tokens_b = roll_in(
        place,
        (own, three, four, other, other_three, other_four),
        ((0, r), (0, 2 * r), (0, r)) * 2,
    )
    via_up_a, via_down_a = send_first(first_products(tokens_a, weights, size))
    via_up_b, via_down_b = send_first(first_products(tokens_b, weights, size))
    up, down = second_products(tokens_a, weights, size, via_up_a, via_down_a)
    below_a, above_a = send_second(up, down)
    up, down = second_products(tokens_b, weights, size, via_up_b, via_down_b)
    tokens_a, up, down = tie(tokens_a, up, down)
    below_b, above_b = send_second(up, down)
    place_a, parts_a = third_products(tokens_a, weights, size, below_a, above_a)
    pair_a = hidden_pair(place_a, parts_a)
    got_a = gather_second(pair_a)
    place_b, parts_b = third_products(tokens_b, weights, size, below_b, above_b)
    line_a = gather_first(pair_a, got_a)
    place_b, line_a = tie(place_b, line_a)
    up_a, down_a = send_line(line_a)
    pair_b = hidden_pair(place_b, parts_b)
    got_b = gather_second(pair_b)
    pair_b, up_a, down_a = tie(pair_b, up_a, down_a)
    far_up_a, far_down_a = send_plane(up_a[0], 0, -1), send_plane(down_a[1], 0, 1)
    line_b = gather_first(pair_b, got_b)
    up_b, down_b = send_line(line_b)
    far_up_b, far_down_b = send_plane(up_b[0], 0, -1), send_plane(down_b[1], 0, 1)
    far_down_a, up_b, down_b = tie(far_down_a, up_b, down_b)
    deltas = [line_a[1], up_a[1], far_down_a, down_a[1]]
    partial = roll_back(place, [last(p, weight_in) for p in deltas], LONG)
    half = 4 * r
    near = partial[:half] + value(swap(code(partial[half:])))
    from_two = send_z(code(near[2 * r :]), -2)
    from_one = send_z(code(near[: 2 * r]), -1)
    deltas_b = [line_b[1], up_b[1], far_down_b, down_b[1]]
    partial = roll_back(place, [last(p, weight_in) for p in deltas_b], SHORT)
    deep = partial[:half] + value(swap(code(partial[half:])))
    deep_three, then = tie(code(deep[r : 3 * r]), deep)
    from_three = send_z(deep_three, -3)
    from_four = send_z(code(then[3 * r :]), -4)
    far_up_a, far_down_a, deep = tie(far_up_a, far_down_a, deep)
    streams = [tokens_a, tokens_b]
    inputs, cots = [t[0] for t in streams], [t[1] for t in streams]
    acts = [line_a[0], up_a[0], far_up_a, down_a[0], line_b[0], up_b[0], far_up_b, down_b[0]]
    deltas[2] = far_down_a
    deltas += deltas_b
    grad_out = grad_kernel(acts, cots, False, factor)
    grad_in = grad_kernel(deltas, inputs, True, factor)
    from_one, from_two, from_three, from_four, grad_out, grad_in = tie(
        from_one, from_two, from_three, from_four, grad_out, grad_in
    )
    pieces = [value(piece) for piece in (from_one, from_two, from_three)]
    others = value(swap(code(sum(piece[r:] for piece in pieces))))
    grad_x = deep[:r] + value(from_four) + sum(piece[:r] for piece in pieces) + others
    return (grad_x, grad_in, grad_out)


def solution(mesh):
    in_specs = (P("col", "row"), P("col", "row"), P("row", "col"), P("col", "row"))
    out_specs = (P("col", "row"), P("row", "col"), P("col", "row"))
    return jax.shard_map(
        on_device, mesh=mesh, in_specs=in_specs, out_specs=out_specs, check_vma=False
    )
```
